1024 devices in a mesh: group: 16 (over y, core), dom: 64 (over z, x).
Axes of the slice: x: 4, y: 8, z: 16, core: 2. Of those that a mesh axis runs over, the one named last changes fastest.
Arguments:
- node_state: bfloat16 [524288, 256], P(('group', 'dom')), may hold values from -6 to 6
- cotangent: bfloat16 [524288, 256], P(('group', 'dom')), may hold values from -6 to 6
- stale_domain: bfloat16 [524288, 256], P(('group', 'dom')), may hold values from -6 to 6
- stale_group: bfloat16 [131072, 256], P(('group', 'dom')), may hold values from -6 to 6
- stale_gradient: bfloat16 [524288, 256], P(('group', 'dom')), may hold values from -4 to 4
- tile_values: bfloat16 [32768, 128, 128], P(('group', 'dom')), may hold values from 0 to 0.1, as said below
- tile_source: int32 [32768], P(('group', 'dom')), may hold values from 0 to 8
- tile_target: int32 [32768], P(('group', 'dom')), may hold values from 0 to 3
- tile_count: int32 [1024], P(('group', 'dom')), may hold values from 4 to 32, as said below
- send_domain: int32 [524288], P(('group', 'dom')), may hold values from 0 to 511
- count_domain: int32 [65536], P(('group', 'dom')), may hold values from 1 to 8, as said below
- send_group: int32 [131072], P(('group', 'dom')), may hold values from 0 to 511
- count_group: int32 [16384], P(('group', 'dom')), may hold values from 1 to 8, as said below
- weight_self: bfloat16 [256, 256], replicated, may hold values from -0.375 to 0.375
- weight_neighbour: bfloat16 [256, 256], replicated, may hold values from -0.375 to 0.375
- bias_vector: float32 [256], replicated, may hold values from -4 to 4
Outputs:
- activation: bfloat16 [524288, 256], P(('group', 'dom'))
- state_gradient: bfloat16 [524288, 256], P(('group', 'dom'))
- next_domain: bfloat16 [524288, 256], P(('group', 'dom'))
- next_group: bfloat16 [131072, 256], P(('group', 'dom'))
- next_gradient: bfloat16 [524288, 256], P(('group', 'dom'))
- grad_self: float32 [256, 256], replicated
- grad_neighbour: float32 [256, 256], replicated
- grad_bias: float32 [256], replicated
The draws below stay inside these ranges and needn't reach their ends.
Inputs may be any that keep to these rules, and one draw needn't show every extreme that they name: `tile_count`: each device's tiles at positions at or above its count are ignored; the counts are 32 divided by 1, 2, 4 or 8, and some device has exactly 32. `count_domain`: counts of live slots toward each partner of the same group; in every group some device receives 8 live rows from every partner. `count_group`: counts of live slots toward each group; for every partition index some device receives 8 live rows from every group. `tile_values`: edge weights, zero for missing edges.
All inputs are finite; a program needn't handle non-finite values.
Results may differ from the reference program's by a relative error of at most 0.0065.
Values may be sent and summed in bfloat16 or wider, within the bound.
No kernel may reach another device: no remote copies, remote signals or barrier semaphores. Data moves between devices by JAX's collectives and lax.ppermute only.
A program may use at most 64 MiB of HBM per device.

```python
import jax
import jax.numpy as jnp
from jax import lax

H = 256
TILE = 128
NODES_DEV = 512
NT_MAX = 32
BND_DOM = 512
BND_GRP = 128
SLOT = 8
SLOTG = 8
NODES = 524288
N_GROUP = 16
N_DOM = 64
DEVICES = 1024


def draw_tile_values(key, part):
    key = jax.random.fold_in(key, 11)
    first, second = jax.random.split(key)
    shape = (DEVICES * NT_MAX, TILE, TILE)
    present = jax.random.randint(first, shape, 0, 8) == 0
    weights = jax.random.uniform(second, shape, jnp.float32, 0.5, 1.5) / 16.0
    return jnp.where(present, weights, jnp.zeros((), jnp.float32)).astype(jnp.bfloat16)


def draw_tile_count(key, part):
    key = jax.random.fold_in(key, 12)
    first, second = jax.random.split(key)
    shifts = jax.random.randint(first, (DEVICES,), 0, 4)
    counts = jnp.right_shift(jnp.full((DEVICES,), NT_MAX, jnp.int32), shifts.astype(jnp.int32))
    chosen = jax.random.randint(second, (), 0, DEVICES)
    return counts.at[chosen].set(NT_MAX).astype(jnp.int32)


def draw_count_domain(key, part):
    key = jax.random.fold_in(key, 13)
    first, second = jax.random.split(key)
    counts = jax.random.randint(first, (N_GROUP, N_DOM, N_DOM), max(1, SLOT // 4), SLOT + 1)
    receiver = jax.random.randint(second, (N_GROUP,), 0, N_DOM)
    full = jnp.arange(N_DOM)[None, None, :] == receiver[:, None, None]
    return jnp.where(full, SLOT, counts).reshape(-1).astype(jnp.int32)


def draw_count_group(key, part):
    key = jax.random.fold_in(key, 14)
    first, second = jax.random.split(key)
    counts = jax.random.randint(first, (N_GROUP, N_DOM, N_GROUP), max(1, SLOTG // 4), SLOTG + 1)
    receiver = jax.random.randint(second, (N_DOM,), 0, N_GROUP)
    full = jnp.arange(N_GROUP)[None, None, :] == receiver[None, :, None]
    return jnp.where(full, SLOTG, counts).reshape(-1).astype(jnp.int32)


def set_ends(array, stream_key, low, high):
    spot = [jax.random.randint(jax.random.fold_in(stream_key, axis), (), 0, length) for axis, length in enumerate(array.shape)]
    widest = array.shape.index(max(array.shape))
    neighbour = spot[:widest] + [(spot[widest] + 1) % array.shape[widest]] + spot[widest + 1:]
    return array.at[tuple(spot)].set(low).at[tuple(neighbour)].set(high)


def levels(own_key, dims, shards, least, largest):
    def one(dim, blocks):
        heights = jax.random.uniform(jax.random.fold_in(jax.random.fold_in(own_key, 6), dim), (blocks,), jnp.float32, least / len(shards), largest / len(shards))
        return jnp.repeat(jnp.exp(heights), dims[dim] // blocks).reshape((-1,) + (1,) * (len(dims) - dim - 1))

    level = one(*shards[0])
    for cut in shards[1:]:
        level = level * one(*cut)
    return level


def gaussian(key, shape, width, most, cuts=(), held_as=jnp.bfloat16):
    entries = width * jax.random.normal(key, shape, jnp.float32)
    if cuts:
        entries = entries * levels(key, shape, cuts, -0.22, 0.18)
    return jnp.clip(entries, -most, most).astype(held_as)


def setup_inputs(seed: int = 0) -> dict:
    arg_keys = jax.random.split(jax.random.key(seed), 17)
    return {
        "node_state": gaussian(arg_keys[0], (NODES, H), 1.0, 6.0, ((0, 1024),)),
        "cotangent": gaussian(arg_keys[1], (NODES, H), 1.0, 6.0, ((0, 1024),)),
        "stale_domain": gaussian(arg_keys[2], (DEVICES * BND_DOM, H), 1.0, 6.0, ((0, 1024),)),
        "stale_group": gaussian(arg_keys[3], (DEVICES * BND_GRP, H), 1.0, 6.0, ((0, 1024),)),
        "stale_gradient": gaussian(arg_keys[4], (NODES, H), 0.5, 4.0, ((0, 1024),)),
        "tile_values": draw_tile_values(jax.random.fold_in(arg_keys[16], 71), 0),
        "tile_source": set_ends(jax.random.randint(arg_keys[6], (DEVICES * NT_MAX,), 0, (NODES_DEV + BND_DOM + BND_GRP) // TILE), jax.random.fold_in(arg_keys[6], 1), 0, ((NODES_DEV + BND_DOM + BND_GRP) // TILE) - 1).astype(jnp.int32),
        "tile_target": set_ends(jax.random.randint(arg_keys[7], (DEVICES * NT_MAX,), 0, NODES_DEV // TILE), jax.random.fold_in(arg_keys[7], 1), 0, (NODES_DEV // TILE) - 1).astype(jnp.int32),
        "tile_count": draw_tile_count(jax.random.fold_in(arg_keys[16], 71), 0),
        "send_domain": set_ends(jax.random.randint(arg_keys[9], (DEVICES * BND_DOM,), 0, NODES_DEV), jax.random.fold_in(arg_keys[9], 1), 0, NODES_DEV - 1).astype(jnp.int32),
        "count_domain": draw_count_domain(jax.random.fold_in(arg_keys[16], 71), 0),
        "send_group": set_ends(jax.random.randint(arg_keys[11], (DEVICES * BND_GRP,), 0, NODES_DEV), jax.random.fold_in(arg_keys[11], 1), 0, NODES_DEV - 1).astype(jnp.int32),
        "count_group": draw_count_group(jax.random.fold_in(arg_keys[16], 71), 0),
        "weight_self": gaussian(arg_keys[13], (H, H), H ** -0.5, 0.375),
        "weight_neighbour": gaussian(arg_keys[14], (H, H), H ** -0.5, 0.375),
        "bias_vector": gaussian(arg_keys[15], (H,), 1.0, 4.0, (), jnp.float32),
    }


def silu_slope(preact):
    sigmoid = jax.nn.sigmoid(preact)
    return sigmoid * (1.0 + preact * (1.0 - sigmoid))


def pack_rows(source, indices, counts):
    per_peer = indices.shape[0] // counts.shape[0]
    filled = (jnp.arange(per_peer)[None, :] < counts[:, None]).reshape(-1)
    return jnp.where(filled[:, None], source[indices], jnp.zeros((), source.dtype))


def spread_rows(totals, arrived, indices, counts):
    per_peer = indices.shape[0] // counts.shape[0]
    filled = (jnp.arange(per_peer)[None, :] < counts[:, None]).reshape(-1)
    addend = jnp.where(filled[:, None], arrived.astype(jnp.float32), jnp.zeros((), jnp.float32))
    return totals.at[indices].add(addend)


def reference(node_state, cotangent, stale_domain, stale_group, stale_gradient, tile_values, tile_source, tile_target, tile_count, send_domain, count_domain, send_group, count_group, weight_self, weight_neighbour, bias_vector):
    device_total = N_GROUP * N_DOM
    highest = lax.Precision.HIGHEST
    own_blocks = NODES_DEV // TILE

    def one_device(running, pieces):
        state, cot_rows, stale_dom_rows, stale_grp_rows, stale_grad_rows, values, source, target, tile_total = pieces
        extended = jnp.concatenate([state, stale_dom_rows, stale_grp_rows], 0).reshape(-1, TILE, H)
        ext_blocks = extended.shape[0]
        active = jnp.arange(NT_MAX) < tile_total
        products = jnp.einsum("kij,kjh->kih", values.astype(jnp.float32), extended[source].astype(jnp.float32), precision=highest)
        target_hit = ((target[None, :] == jnp.arange(own_blocks)[:, None]) & active[None, :]).astype(jnp.float32)
        gathered = jnp.einsum("bk,kih->bih", target_hit, products, precision=highest).reshape(NODES_DEV, H).astype(jnp.bfloat16)
        preact = jnp.dot(state, weight_self, preferred_element_type=jnp.float32) + jnp.dot(gathered, weight_neighbour, preferred_element_type=jnp.float32) + bias_vector
        activation = jax.nn.silu(preact).astype(jnp.bfloat16)
        pre_grad = (cot_rows.astype(jnp.float32) * silu_slope(preact)).astype(jnp.bfloat16)
        sum_self = running[0] + jnp.dot(state.T, pre_grad, preferred_element_type=jnp.float32)
        sum_neigh = running[1] + jnp.dot(gathered.T, pre_grad, preferred_element_type=jnp.float32)
        sum_bias = running[2] + jnp.sum(pre_grad.astype(jnp.float32), 0)
        agg_grad = jnp.dot(pre_grad, weight_neighbour.T, preferred_element_type=jnp.float32).astype(jnp.bfloat16).reshape(own_blocks, TILE, H)
        returned = jnp.einsum("kij,kih->kjh", values.astype(jnp.float32), agg_grad[target].astype(jnp.float32), precision=highest)
        source_hit = ((source[None, :] == jnp.arange(ext_blocks)[:, None]) & active[None, :]).astype(jnp.float32)
        ext_grad = jnp.einsum("ek,kjh->ejh", source_hit, returned, precision=highest).reshape(-1, H)
        state_grad = (jnp.dot(pre_grad, weight_self.T, preferred_element_type=jnp.float32) + ext_grad[:NODES_DEV] + stale_grad_rows.astype(jnp.float32)).astype(jnp.bfloat16)
        back_dom = ext_grad[NODES_DEV:NODES_DEV + BND_DOM].astype(jnp.bfloat16)
        back_grp = ext_grad[NODES_DEV + BND_DOM:].astype(jnp.bfloat16)
        return (sum_self, sum_neigh, sum_bias), (activation, state_grad, back_dom, back_grp)

    pieces = (node_state.reshape(device_total, NODES_DEV, H), cotangent.reshape(device_total, NODES_DEV, H),
              stale_domain.reshape(device_total, BND_DOM, H), stale_group.reshape(device_total, BND_GRP, H),
              stale_gradient.reshape(device_total, NODES_DEV, H), tile_values.reshape(device_total, NT_MAX, TILE, TILE),
              tile_source.reshape(device_total, NT_MAX), tile_target.reshape(device_total, NT_MAX), tile_count)
    start = (jnp.zeros((H, H), jnp.float32), jnp.zeros((H, H), jnp.float32), jnp.zeros((H,), jnp.float32))
    sums, outputs = lax.scan(one_device, start, pieces)
    activation, state_gradient, back_domain, back_group = outputs

    state_rows = node_state.reshape(device_total, NODES_DEV, H)
    dom_lists = send_domain.reshape(device_total, BND_DOM)
    dom_counts = count_domain.reshape(device_total, N_DOM)
    grp_lists = send_group.reshape(device_total, BND_GRP)
    grp_counts = count_group.reshape(device_total, N_GROUP)
    packed_dom = jax.vmap(pack_rows)(state_rows, dom_lists, dom_counts)
    packed_grp = jax.vmap(pack_rows)(state_rows, grp_lists, grp_counts)
    next_domain = packed_dom.reshape(N_GROUP, N_DOM, N_DOM, SLOT, H).transpose(0, 2, 1, 3, 4).reshape(device_total * BND_DOM, H)
    next_group = packed_grp.reshape(N_GROUP, N_DOM, N_GROUP, SLOTG, H).transpose(2, 1, 0, 3, 4).reshape(device_total * BND_GRP, H)
    arrived_dom = back_domain.reshape(N_GROUP, N_DOM, N_DOM, SLOT, H).transpose(0, 2, 1, 3, 4).reshape(device_total, BND_DOM, H)
    arrived_grp = back_group.reshape(N_GROUP, N_DOM, N_GROUP, SLOTG, H).transpose(2, 1, 0, 3, 4).reshape(device_total, BND_GRP, H)

    def arrive(from_dom, from_grp, dom_list, dom_count, grp_list, grp_count):
        totals = jnp.zeros((NODES_DEV, H), jnp.float32)
        totals = spread_rows(totals, from_dom, dom_list, dom_count)
        totals = spread_rows(totals, from_grp, grp_list, grp_count)
        return totals.astype(jnp.bfloat16)

    next_gradient = jax.vmap(arrive)(arrived_dom, arrived_grp, dom_lists, dom_counts, grp_lists, grp_counts)
    return (activation.reshape(NODES, H), state_gradient.reshape(NODES, H), next_domain, next_group,
            next_gradient.reshape(NODES, H), sums[0] / NODES, sums[1] / NODES, sums[2] / NODES)
```

```python
import functools

import jax
import jax.numpy as jnp
from jax import lax
from jax.experimental import pallas as pl
from jax.experimental.pallas import tpu as pltpu
from jax.sharding import Mesh
from jax.sharding import PartitionSpec as P

F32 = jnp.float32
BF16 = jnp.bfloat16
VMEM = pl.BlockSpec(memory_space=pltpu.VMEM)
SMEM = pl.BlockSpec(memory_space=pltpu.SMEM)
UNROLL = 4
EXTRA = 8
X_SIZE = 4
CONTRACT_FIRST = (((0,), (0,)), ((), ()))
CONTRACT_LAST = (((1,), (1,)), ((), ()))


def kernel_params():
    return pltpu.CompilerParams(vmem_limit_bytes=48 * 1024 * 1024)


def dot(left, right):
    return jnp.dot(left, right, preferred_element_type=F32)


def slot_matrix(indices, counts, rows):
    slots = indices.shape[1]
    peers = counts.shape[1]
    per_peer = slots // peers
    peer = lax.broadcasted_iota(jnp.int32, (peers, slots), 0)
    slot = lax.broadcasted_iota(jnp.int32, (peers, slots), 1)
    owner = (slot // per_peer == peer).astype(F32)
    limit = dot(jnp.broadcast_to(counts.astype(F32), (8, peers)), owner)[0:1]
    place = lax.broadcasted_iota(jnp.int32, (1, slots), 1) % per_peer
    named = jnp.where(place.astype(F32) < limit, indices, -1)
    row = lax.broadcasted_iota(jnp.int32, (rows, slots), 0)
    return (row == named).astype(F32).astype(BF16)


def layer_kernel(
    source,
    target,
    count,
    state,
    cotangent,
    stale_domain,
    stale_group,
    stale_gradient,
    tiles,
    send_domain,
    count_domain,
    send_group,
    count_group,
    weight_self,
    weight_neighbour,
    bias,
    activation,
    state_gradient,
    out_domain,
    out_group,
    partial,
    extended,
    gathered,
    agg,
    ext_grad,
):
    nodes, width = state.shape
    tile = tiles.shape[1]
    own = nodes // tile
    dom_blocks = stale_domain.shape[0] // tile
    for b in range(own):
        extended[b] = state[b * tile : (b + 1) * tile, :]
    for b in range(dom_blocks):
        extended[own + b] = stale_domain[b * tile : (b + 1) * tile, :]
    for b in range(stale_group.shape[0] // tile):
        extended[own + dom_blocks + b] = stale_group[b * tile : (b + 1) * tile, :]
    gathered[...] = jnp.zeros_like(gathered)
    ext_grad[...] = jnp.zeros_like(ext_grad)
    rounds = count[0] // UNROLL

    def gather_tiles(i, carry):
        for u in range(UNROLL):
            k = i * UNROLL + u
            gathered[target[k]] += dot(tiles[k], extended[source[k]])
        return carry

    lax.fori_loop(0, rounds, gather_tiles, 0)
    around = gathered[...].reshape(nodes, width).astype(BF16)
    own_rows = state[...]
    preact = dot(own_rows, weight_self[...]) + dot(around, weight_neighbour[...]) + bias[...]
    sigmoid = jax.nn.sigmoid(preact)
    activation[...] = (preact * sigmoid).astype(BF16)
    slope = sigmoid * (1.0 + preact * (1.0 - sigmoid))
    pre_grad = (cotangent[...].astype(F32) * slope).astype(BF16)

    grads = jnp.concatenate(
        [
            lax.dot_general(own_rows, pre_grad, CONTRACT_FIRST, preferred_element_type=F32),
            lax.dot_general(around, pre_grad, CONTRACT_FIRST, preferred_element_type=F32),
        ],
        0,
    )
    column = jnp.sum(pre_grad.astype(F32), 0, keepdims=True)
    chunks, chunk_rows, lanes = partial.shape
    body = chunk_rows - EXTRA
    parts = width // lanes
    halves = [grads[:, h * lanes : (h + 1) * lanes].reshape(-1, body, lanes) for h in range(parts)]
    extra = jnp.concatenate(
        [column[:, h * lanes : (h + 1) * lanes] for h in range(parts)]
        + [jnp.zeros((EXTRA - parts, lanes), F32)],
        0,
    )
    partial[...] = jnp.concatenate(
        [
            jnp.concatenate(halves, 0),
            jnp.broadcast_to(extra[None], (chunks, EXTRA, lanes)),
        ],
        1,
    ).astype(BF16)

    agg[...] = (
        lax.dot_general(pre_grad, weight_neighbour[...], CONTRACT_LAST, preferred_element_type=F32)
        .astype(BF16)
        .reshape(own, tile, width)
    )

    def return_tiles(i, carry):
        for u in range(UNROLL):
            k = i * UNROLL + u
            ext_grad[source[k]] += lax.dot_general(
                tiles[k], agg[target[k]], CONTRACT_FIRST, preferred_element_type=F32
            )
        return carry

    lax.fori_loop(0, rounds, return_tiles, 0)
    own_term = lax.dot_general(
        pre_grad, weight_self[...], CONTRACT_LAST, preferred_element_type=F32
    )
    state_gradient[...] = (
        own_term + ext_grad[0:own].reshape(nodes, width) + stale_gradient[...].astype(F32)
    ).astype(BF16)

    def packed(indices, counts, back, peers):
        named = slot_matrix(indices[...], counts[...], nodes)
        rows = lax.dot_general(named, own_rows, CONTRACT_FIRST, preferred_element_type=F32)
        return jnp.concatenate(
            [rows.reshape(peers, -1, width), back.reshape(peers, -1, width)], 1
        ).astype(BF16)

    out_domain[...] = packed(
        send_domain, count_domain, ext_grad[own : own + dom_blocks], out_domain.shape[0]
    )
    out_group[...] = packed(
        send_group, count_group, ext_grad[own + dom_blocks :], out_group.shape[0]
    )


def sum_kernel(arrived, spread):
    total = jnp.sum(arrived[...].astype(F32), 0)
    spread[...] = jnp.broadcast_to(total[None], spread.shape).astype(BF16)


def total_kernel(scale, arrived, spread, grad_bias):
    total = jnp.sum(arrived[...].astype(F32), 0) * scale
    body = spread.shape[1]
    spread[...] = jnp.broadcast_to(total[None, 0:body], spread.shape).astype(BF16)
    grad_bias[...] = total[body : body + grad_bias.shape[0]]


def finish_kernel(arrived, grad_self, grad_neighbour):
    lanes = arrived.shape[2]
    rows, width = grad_self.shape
    parts = width // lanes
    per = arrived.shape[0] // parts
    for h in range(parts):
        part = arrived[h * per : (h + 1) * per].astype(F32).reshape(2 * rows, lanes)
        grad_self[:, h * lanes : (h + 1) * lanes] = part[0:rows]
        grad_neighbour[:, h * lanes : (h + 1) * lanes] = part[rows:]


def spread_kernel(
    from_domain,
    from_group,
    send_domain,
    count_domain,
    send_group,
    count_group,
    next_domain,
    next_group,
    next_gradient,
):
    nodes, width = next_gradient.shape

    def split(arrived):
        rows = arrived[...].astype(F32)
        half = rows.shape[1] // 2
        return (
            rows[:, :half].reshape(-1, width).astype(BF16),
            rows[:, half:].reshape(-1, width).astype(BF16),
        )

    inputs, grads = split(from_domain)
    next_domain[...] = inputs
    total = dot(slot_matrix(send_domain[...], count_domain[...], nodes), grads)
    inputs, grads = split(from_group)
    next_group[...] = inputs
    total += dot(slot_matrix(send_group[...], count_group[...], nodes), grads)
    next_gradient[...] = total.astype(BF16)


def struct(shape, dtype):
    return jax.ShapeDtypeStruct(shape, dtype)


def local(
    node_state,
    cotangent,
    stale_domain,
    stale_group,
    stale_gradient,
    tile_values,
    tile_source,
    tile_target,
    tile_count,
    send_domain,
    count_domain,
    send_group,
    count_group,
    weight_self,
    weight_neighbour,
    bias_vector,
):
    nodes, width = node_state.shape
    tile = tile_values.shape[1]
    own = nodes // tile
    domain_rows, group_rows = stale_domain.shape[0], stale_group.shape[0]
    blocks = own + (domain_rows + group_rows) // tile
    dom_peers, group_peers = count_domain.shape[0], count_group.shape[0]
    near = lax.axis_size("group") * lax.axis_size("x")
    far = lax.axis_size("z")
    lanes = 128
    body = 2 * width * width // (near * lanes)
    all_nodes = nodes * near * far
    lists = (
        send_domain.reshape(1, -1),
        count_domain.reshape(1, -1),
        send_group.reshape(1, -1),
        count_group.reshape(1, -1),
    )
    activation, state_gradient, out_domain, out_group, partial = pl.pallas_call(
        layer_kernel,
        out_shape=(
            struct((nodes, width), BF16),
            struct((nodes, width), BF16),
            struct((dom_peers, 2 * domain_rows // dom_peers, width), BF16),
            struct((group_peers, 2 * group_rows // group_peers, width), BF16),
            struct((near, body + EXTRA, lanes), BF16),
        ),
        in_specs=[SMEM] * 3 + [VMEM] * 13,
        out_specs=[VMEM] * 5,
        scratch_shapes=[
            pltpu.VMEM((blocks, tile, width), BF16),
            pltpu.VMEM((own, tile, width), F32),
            pltpu.VMEM((own, tile, width), BF16),
            pltpu.VMEM((blocks, tile, width), F32),
        ],
        compiler_params=kernel_params(),
        name="layer",
    )(
        tile_source,
        tile_target,
        tile_count,
        node_state,
        cotangent,
        stale_domain,
        stale_group,
        stale_gradient,
        tile_values,
        *lists,
        weight_self,
        weight_neighbour,
        bias_vector.reshape(1, -1),
    )

    arrived = lax.all_to_all(partial, ("group", "x"), 0, 0, tiled=True)
    from_domain = lax.all_to_all(out_domain, ("z", "x"), 0, 0, tiled=True)
    from_group = lax.all_to_all(out_group, "group", 0, 0, tiled=True)
    near_sum = pl.pallas_call(
        sum_kernel,
        out_shape=struct((far, body + EXTRA, lanes), BF16),
        in_specs=[VMEM],
        out_specs=VMEM,
        compiler_params=kernel_params(),
        name="near_sum",
    )(arrived)
    arrived = lax.all_to_all(near_sum, "z", 0, 0, tiled=True)
    total, grad_bias = pl.pallas_call(
        functools.partial(total_kernel, 1.0 / all_nodes),
        out_shape=(struct((near, body, lanes), BF16), struct((width // lanes, lanes), F32)),
        in_specs=[VMEM],
        out_specs=[VMEM] * 2,
        compiler_params=kernel_params(),
        name="total",
    )(arrived)
    arrived = lax.all_to_all(total, ("group", "x"), 0, 0, tiled=True)
    grad_self, grad_neighbour = pl.pallas_call(
        finish_kernel,
        out_shape=(struct((width, width), F32), struct((width, width), F32)),
        in_specs=[VMEM],
        out_specs=[VMEM] * 2,
        compiler_params=kernel_params(),
        name="finish",
    )(arrived)
    next_domain, next_group, next_gradient = pl.pallas_call(
        spread_kernel,
        out_shape=(
            struct((domain_rows, width), BF16),
            struct((group_rows, width), BF16),
            struct((nodes, width), BF16),
        ),
        in_specs=[VMEM] * 6,
        out_specs=[VMEM] * 3,
        compiler_params=kernel_params(),
        name="spread",
    )(from_domain, from_group, *lists)
    return (
        activation,
        state_gradient,
        next_domain,
        next_group,
        next_gradient,
        grad_self,
        grad_neighbour,
        grad_bias.reshape(-1),
    )


def solution(mesh):
    groups, domains = mesh.devices.shape
    x_size = X_SIZE if domains > X_SIZE else 2
    fine = Mesh(mesh.devices.reshape(groups, domains // x_size, x_size), ("group", "z", "x"))
    every = ("group", "z", "x")
    rows, vector, copied = P(every, None), P(every), P()
    return jax.shard_map(
        local,
        mesh=fine,
        in_specs=(rows,) * 5
        + (P(every, None, None),)
        + (vector,) * 7
        + (copied,) * 3,
        out_specs=(rows,) * 5 + (copied,) * 3,
        check_vma=False,
    )
```
